32 devices in a mesh: layer: 2 (over core), dict: 16 (over z, y, x).
Axes of the slice: x: 2, y: 2, z: 4, core: 2. Of those that a mesh axis runs over, the one named last changes fastest.
Arguments:
- hidden: bfloat16 [2, 512, 9216], P('layer', None, 'dict'), may hold values from -6 to 6
- row_list: int32 [512], replicated, may hold values from 0 to 511, each once
- w_down: bfloat16 [2, 9216, 2304], P('layer', 'dict'), may hold values from -0.0625 to 0.0625
- w_enc: bfloat16 [2, 2304, 8192], P('layer', None, 'dict'), may hold values from -0.09375 to 0.09375
- b_enc: float32 [8192], P('dict'), may hold values from -3 to 3
- w_dec: float32 [2, 8192, 2304], P('layer', 'dict'), may hold values from -0.0625 to 0.0625
- b_dec: float32 [2, 2304], P('layer'), may hold values from -3 to 3
- alive_mask: int32 [8192], P('dict'), may hold values 0 or 1
Outputs:
- latent: bfloat16 [512, 8192], P('layer', 'dict')
- residual: float32 [2, 512, 2304], P('layer', 'dict')
- adjoint: float32 [512, 8192], P('layer', 'dict')
The draws below stay inside these ranges and needn't reach their ends.
Inputs may be any that keep to these rules, and one draw needn't show every extreme that they name: `row_list`: a permutation of the 512 buffer rows.
All inputs are finite; a program needn't handle non-finite values. No bound on the sum of `alive_mask` on one device may be relied on, other than what follows from the above.
Results may differ from the reference program's by a relative error of at most 0.0045.
Values may be sent and summed in bfloat16 or wider, within the bound.
A program may use at most 64 MiB of HBM per device.

```python
import jax
import jax.numpy as jnp
from jax import lax

D = 2304
FF = 9216
ROWS = 512
LAYERS = 2
LATENTS = 8192


def plant(entries, stream_key, smallest, high):
    index_at = [jax.random.randint(jax.random.fold_in(stream_key, axis), (), 0, length) for axis, length in enumerate(entries.shape)]
    main_axis = entries.shape.index(max(entries.shape))
    beside = index_at[:main_axis] + [(index_at[main_axis] + 1) % entries.shape[main_axis]] + index_at[main_axis + 1:]
    return entries.at[tuple(index_at)].set(smallest).at[tuple(beside)].set(high)


def level_of(key, extent, cuts, low, high):
    level, own = 1.0, jax.random.fold_in(key, 6)
    for position, blocks in cuts:
        steps = jnp.exp(jax.random.uniform(jax.random.fold_in(own, position), (blocks,), jnp.float32, low / len(cuts), high / len(cuts)))
        level = level * jnp.repeat(steps, extent[position] // blocks).reshape([-1 if axis == position else 1 for axis in range(len(extent))])
    return level


def noise(own_key, shape, width, most, split=(), held_as=jnp.bfloat16):
    gain = level_of(own_key, shape, split, -0.22, 0.18) if split else 1.0
    array = jax.random.normal(own_key, shape, jnp.float32) * width * gain
    return jnp.minimum(jnp.maximum(array, -most), most).astype(held_as)


def setup_inputs(seed: int = 0) -> dict:
    streams_of = jax.random.split(jax.random.key(seed), 9)
    hidden = noise(streams_of[0], (LAYERS, ROWS, FF), 1.0, 6.0, ((0, 2), (2, 16)))
    row_list = jax.random.permutation(streams_of[1], ROWS).astype(jnp.int32)
    w_down = noise(streams_of[2], (LAYERS, FF, D), FF ** -0.5, 0.0625, ((0, 2), (1, 16)))
    w_enc = noise(streams_of[3], (LAYERS, D, LATENTS), (D * LAYERS) ** -0.5, 0.09375, ((0, 2), (2, 16)))
    b_enc = noise(streams_of[4], (LATENTS,), 0.5, 3.0, ((0, 16),), jnp.float32)
    w_dec = noise(streams_of[5], (LAYERS, LATENTS, D), LATENTS ** -0.5, 0.0625, ((0, 2), (1, 16)), jnp.float32)
    b_dec = noise(streams_of[6], (LAYERS, D), 0.5, 3.0, ((0, 2),), jnp.float32)
    alive_mask = plant((jax.random.randint(streams_of[7], (LATENTS,), 0, 8) < 7).astype(jnp.int32), jax.random.fold_in(streams_of[7], 1), 0, 1)
    return dict(hidden=hidden, row_list=row_list, w_down=w_down, w_enc=w_enc, b_enc=b_enc, w_dec=w_dec, b_dec=b_dec, alive_mask=alive_mask)


def reference(hidden, row_list, w_down, w_enc, b_enc, w_dec, b_dec, alive_mask):
    alive_float = alive_mask.astype(jnp.float32)
    activations = []
    preact = jnp.zeros((ROWS, LATENTS), jnp.float32) + b_enc.astype(jnp.float32)
    for source in range(LAYERS):
        chosen = jnp.take(hidden[source], row_list, axis=0)
        produced = jnp.dot(chosen, w_down[source], preferred_element_type=jnp.float32).astype(jnp.bfloat16)
        activations.append(produced)
        preact = preact + jnp.dot(produced, w_enc[source], preferred_element_type=jnp.float32)
    latent = (jnp.maximum(preact, 0.0) * alive_float).astype(jnp.bfloat16)
    latent_wide = latent.astype(jnp.float32)
    residuals = []
    summed = jnp.zeros((ROWS, LATENTS), jnp.float32)
    for source in range(LAYERS):
        rebuilt = jnp.dot(latent_wide, w_dec[source], precision=lax.Precision.HIGHEST, preferred_element_type=jnp.float32) + b_dec[source]
        remainder = activations[source].astype(jnp.float32) - rebuilt
        residuals.append(remainder)
        summed = summed + jnp.dot(remainder, w_dec[source].T, precision=lax.Precision.HIGHEST, preferred_element_type=jnp.float32)
    adjoint = -summed * alive_float
    return latent, jnp.stack(residuals), adjoint
```

```python
import functools
import math

import jax
import jax.numpy as jnp
from jax import lax
from jax.experimental import pallas as pl
from jax.experimental.pallas import tpu as pltpu
from jax.sharding import PartitionSpec as P

F32, BF16, I32 = jnp.float32, jnp.bfloat16, jnp.int32
PARTS = 2


def digits_of(mesh):
    line = list(mesh.devices.reshape(mesh.shape["layer"], -1)[0])
    count = len(line)
    try:
        coords = [tuple(d.coords) for d in line]
    except (AttributeError, TypeError):
        coords = None
    sizes = []
    if coords:
        found = []
        for axis in range(len(coords[0])):
            values = [c[axis] for c in coords]
            size = len(set(values))
            if size > 1:
                stride = next(i for i in range(count) if values[i] != values[0])
                found.append((stride, size))
        sizes = [size for _, size in sorted(found, reverse=True)]
    if math.prod(sizes) != count or len(sizes) > 3:
        sizes = [count // 4, 2, 2] if count % 4 == 0 else [count]
    return tuple([1] * (3 - len(sizes)) + sizes)


def kernel(dims, layers, batches, share, depth, width, latents, names, *refs):
    ref = dict(zip(names, refs))
    count = math.prod(dims)
    part = width // PARTS
    tile = part // 3 if part % 384 == 0 else part
    tiles = part // tile
    rows = count * share
    per_layer = count // layers
    layer, place = lax.axis_index("layer"), lax.axis_index("dict")
    mine = (place // (dims[1] * dims[2]), place // dims[2] % dims[1], place % dims[2])
    strides = (dims[1] * dims[2], dims[2], 1)
    orders = ((2, 1, 0), (1, 2, 0))

    def peer_of(axis, step):
        other = lax.rem(mine[axis] + step, dims[axis])
        return other, (layer, place + (other - mine[axis]) * strides[axis])

    def layer_peer(step):
        other = lax.rem(layer + step, layers)
        return other, (other, place)

    used = [0]

    def send(src, dst, device):
        slot = used[0]
        used[0] += 1
        copy = pltpu.make_async_remote_copy(
            src_ref=src,
            dst_ref=dst,
            send_sem=ref["send"].at[slot],
            recv_sem=ref["recv"].at[slot],
            device_id=device,
            device_id_type=pl.DeviceIdType.MESH,
        )
        copy.start()
        return copy

    loads = {}
    for slot, name in enumerate(("hidden", "w_down", "w_enc", "w_dec")):
        loads[name] = pltpu.make_async_copy(ref[name].at[0], ref[name + "_v"], ref["load"].at[slot])
        loads[name].start()

    barrier = pltpu.get_barrier_semaphore()
    peers = [peer_of(axis, step)[1] for axis in range(3) for step in range(1, dims[axis])]
    peers += [layer_peer(step)[1] for step in range(1, layers)]
    for device in peers:
        pl.semaphore_signal(barrier, inc=1, device_id=device, device_id_type=pl.DeviceIdType.MESH)

    at = lax.broadcasted_iota(I32, (count * batches * share,) * 2, 0)
    picked = jnp.where(at == ref["row_list"][...], 1.0, 0.0).T.astype(BF16)
    loads["hidden"].wait()
    chosen = jnp.dot(picked, ref["hidden_v"][...], preferred_element_type=F32).astype(BF16)
    ref["chosen"][...] = chosen.reshape(count, batches, share, depth)
    loads["w_down"].wait()
    pl.semaphore_wait(barrier, len(peers))

    def whole(axes):
        return tuple(pl.ds(mine[a], 1) if a in axes else slice(None) for a in range(3))

    def spread(b, c, phase, product):
        wide, narrow = ref[f"wide{b}{c}"], ref[f"narrow{b}{c}{phase}"]

        def step(j, carry):
            at = pl.multiple_of(j * tile, 128)
            value = product(pl.multiple_of(c * part + at, 128)).reshape(dims + (share, tile))
            wide[:, :, :, :, pl.ds(at, tile)] = value
            narrow[:, :, :, :, pl.ds(at, tile)] = value.astype(BF16)
            return carry

        lax.fori_loop(0, tiles, step, 0)
        return send_stage(b, c, phase, 0, narrow)

    def send_stage(b, c, phase, stage, source):
        axis = orders[c][stage]
        copies = []
        for step in range(1, dims[axis]):
            other, device = peer_of(axis, step)
            index = tuple(pl.ds(other, 1) if a == axis else slice(None) for a in range(3))
            copies.append(send(source.at[index], ref[f"in{b}{c}{phase}{stage}"].at[step - 1], device))
        return copies

    def add_stage(b, c, phase, stage, copies):
        axis = orders[c][stage]
        own = ref[f"wide{b}{c}"] if stage == 0 else ref[f"sum{b}{c}{stage - 1}"]
        index = tuple(pl.ds(mine[a], 1) if a == axis else slice(None) for a in range(3))
        for copy in copies:
            copy.wait_recv()
        total = own[index]
        for step in range(dims[axis] - 1):
            total = total + ref[f"in{b}{c}{phase}{stage}"][step].astype(F32)
        return total

    def reduce_rows(b, phase, copies, sent):
        for stage in range(2):
            yield
            following = []
            for c in range(PARTS):
                total = add_stage(b, c, phase, stage, copies[c])
                ref[f"sum{b}{c}{stage}"][...] = total
                out = ref[f"out{b}{c}{phase}{stage}"]
                out[...] = total.astype(BF16)
                following.append(send_stage(b, c, phase, stage + 1, out))
            sent += copies[0] + copies[1]
            copies = following
        yield
        sent += copies[0] + copies[1]
        return [add_stage(b, c, phase, 2, copies[c]) for c in range(PARTS)]

    def gather_stage(b, c, phase, stage):
        axes = [orders[c][s] for s in range(stage + 1)]
        block = ref[f"all{b}{c}{phase}"].at[whole(axes)]
        axis = orders[c][stage]
        return [send(block, block, peer_of(axis, step)[1]) for step in range(1, dims[axis])]

    def gather_rows(b, phase, copies, sent):
        for stage in (1, 0):
            yield
            following = []
            for c in range(PARTS):
                for copy in copies[c]:
                    copy.wait_recv()
                following.append(gather_stage(b, c, phase, stage))
            sent += copies[0] + copies[1]
            copies = following
        yield
        for c in range(PARTS):
            for copy in copies[c]:
                copy.wait_recv()
        sent += copies[0] + copies[1]

    alive = ref["alive"][...].astype(F32)

    def chain(b, sent):
        lhs = ref["chosen"][:, b].reshape(rows, depth)
        copies = [
            spread(b, c, 0, lambda at: jnp.dot(lhs, ref["w_down_v"][:, pl.ds(at, tile)], preferred_element_type=F32))
            for c in range(PARTS)
        ]
        if b == batches - 1:
            loads["w_dec"].wait()

            def split(i, carry):
                at = pl.ds(pl.multiple_of(i * 64, 64), 64)
                value = ref["w_dec_v"][at, :]
                high = value.astype(BF16)
                ref["high"][at, :] = high
                ref["low"][at, :] = (value - high.astype(F32)).astype(BF16)
                return carry

            lax.fori_loop(0, latents // 64, split, 0)
            loads["w_enc"].wait()
        totals = yield from reduce_rows(b, 0, copies, sent)
        copies = []
        for c in range(PARTS):
            ref[f"all{b}{c}0"][whole((0, 1, 2))] = totals[c].astype(BF16)
            copies.append(gather_stage(b, c, 0, 2))
        yield from gather_rows(b, 0, copies, sent)
        encoded = ref[f"encoded{b}"]
        for c in range(PARTS):
            acts = ref[f"all{b}{c}0"][...].reshape(rows, part)
            term = jnp.dot(acts, ref["w_enc_v"][c * part:(c + 1) * part, :], preferred_element_type=F32)
            encoded[...] = term if c == 0 else encoded[...] + term
        copies = [send(encoded, ref[f"encoded_in{b}"].at[s - 1], layer_peer(s)[1]) for s in range(1, layers)]
        yield
        for copy in copies:
            copy.wait_recv()
        sent += copies
        preact = encoded[...]
        for s in range(layers - 1):
            preact = preact + ref[f"encoded_in{b}"][s]
        preact = preact + ref["b_enc"][...]
        latent = (jnp.maximum(preact, 0.0) * alive).astype(BF16)
        ref[f"latent{b}"][...] = latent.reshape(count, share, latents)
        ref["latent_out"][:, b] = ref[f"latent{b}"][pl.ds(layer * per_layer, per_layer)]

        def decode(at):
            left = ref[f"latent{b}"][...].reshape(rows, latents)
            return jnp.dot(left, ref["high"][:, pl.ds(at, tile)], preferred_element_type=F32) + jnp.dot(
                left, ref["low"][:, pl.ds(at, tile)], preferred_element_type=F32
            )

        copies = [spread(b, c, 1, decode) for c in range(PARTS)]
        totals = yield from reduce_rows(b, 1, copies, sent)
        copies = []
        for c in range(PARTS):
            own = ref[f"all{b}{c}0"][whole((0, 1, 2))].reshape(share, part).astype(F32)
            columns = slice(c * part, (c + 1) * part)
            residual = own - (totals[c].reshape(share, part) + ref["b_dec"][:, columns])
            ref["residual_out"][b, :, columns] = residual
            ref[f"all{b}{c}1"][whole((0, 1, 2))] = residual.astype(BF16).reshape(1, 1, 1, share, part)
            copies.append(gather_stage(b, c, 1, 2))
        yield from gather_rows(b, 1, copies, sent)
        back = ref[f"back{b}"]
        for c in range(PARTS):
            left = ref[f"all{b}{c}1"][...].reshape(rows, part)
            columns = slice(c * part, (c + 1) * part)
            contract = (((1,), (1,)), ((), ()))
            term = lax.dot_general(left, ref["high"][:, columns], contract, preferred_element_type=F32)
            term = term + lax.dot_general(left, ref["low"][:, columns], contract, preferred_element_type=F32)
            term = term.reshape(count, share, latents)
            back[...] = term if c == 0 else back[...] + term
        copies = []
        for s in range(1, layers):
            other, device = layer_peer(s)
            block = back.at[pl.ds(other * per_layer, per_layer)]
            copies.append(send(block, ref[f"back_in{b}"].at[s - 1], device))
        yield
        for copy in copies:
            copy.wait_recv()
        sent += copies
        total = back[pl.ds(layer * per_layer, per_layer)]
        for s in range(layers - 1):
            total = total + ref[f"back_in{b}"][s]
        ref["adjoint_out"][:, b] = -total * alive[None]

    sent = []
    running = [chain(b, sent) for b in range(batches)]
    while running:
        for item in list(running):
            if next(item, running) is running:
                running.remove(item)
    for copy in sent:
        copy.wait_send()


def per_device(dims, layers, hidden, row_list, w_down, w_enc, b_enc, w_dec, b_dec, alive_mask):
    count = math.prod(dims)
    _, row_count, depth = hidden.shape
    width, latents = w_enc.shape[1:]
    part = width // PARTS
    batches = 2 if row_count // count % 32 == 0 else 1
    share = row_count // count // batches
    rows = count * share
    orders = ((2, 1, 0), (1, 2, 0))

    scratch = {
        "hidden_v": pltpu.VMEM((row_count, depth), BF16),
        "w_down_v": pltpu.VMEM((depth, width), BF16),
        "w_enc_v": pltpu.VMEM((width, latents), BF16),
        "w_dec_v": pltpu.VMEM((latents, width), F32),
        "high": pltpu.VMEM((latents, width), BF16),
        "low": pltpu.VMEM((latents, width), BF16),
        "chosen": pltpu.VMEM((count, batches, share, depth), BF16),
    }
    for b in range(batches):
        scratch[f"encoded{b}"] = pltpu.VMEM((rows, latents), F32)
        scratch[f"encoded_in{b}"] = pltpu.VMEM((max(layers - 1, 1), rows, latents), F32)
        scratch[f"latent{b}"] = pltpu.VMEM((count, share, latents), BF16)
        scratch[f"back{b}"] = pltpu.VMEM((count, share, latents), F32)
        scratch[f"back_in{b}"] = pltpu.VMEM((max(layers - 1, 1), count // layers, share, latents), F32)
        for c in range(PARTS):
            scratch[f"wide{b}{c}"] = pltpu.VMEM(dims + (share, part), F32)
            for phase in range(2):
                scratch[f"narrow{b}{c}{phase}"] = pltpu.VMEM(dims + (share, part), BF16)
                scratch[f"all{b}{c}{phase}"] = pltpu.VMEM(dims + (share, part), BF16)
            left = list(dims)
            for stage, axis in enumerate(orders[c]):
                steps = max(left[axis] - 1, 1)
                left[axis] = 1
                for phase in range(2):
                    scratch[f"in{b}{c}{phase}{stage}"] = pltpu.VMEM((steps, *left, share, part), BF16)
                    if stage < 2:
                        scratch[f"out{b}{c}{phase}{stage}"] = pltpu.VMEM((*left, share, part), BF16)
                if stage < 2:
                    scratch[f"sum{b}{c}{stage}"] = pltpu.VMEM((*left, share, part), F32)
    copies = 4 * batches * PARTS * sum(d - 1 for d in dims) + 2 * batches * (layers - 1)
    scratch["load"] = pltpu.SemaphoreType.DMA((4,))
    scratch["send"] = pltpu.SemaphoreType.DMA((copies,))
    scratch["recv"] = pltpu.SemaphoreType.DMA((copies,))

    names = ("hidden", "w_down", "w_enc", "w_dec", "row_list", "b_enc", "b_dec", "alive")
    names += ("latent_out", "residual_out", "adjoint_out") + tuple(scratch)
    vmem = pl.BlockSpec(memory_space=pltpu.VMEM)
    hbm = pl.BlockSpec(memory_space=pl.ANY)
    own = (count // layers, batches, share, latents)
    latent, residual, adjoint = pl.pallas_call(
        functools.partial(kernel, dims, layers, batches, share, depth, width, latents, names),
        out_shape=(
            jax.ShapeDtypeStruct(own, BF16),
            jax.ShapeDtypeStruct((batches, share, width), F32),
            jax.ShapeDtypeStruct(own, F32),
        ),
        in_specs=[hbm] * 4 + [vmem] * 4,
        out_specs=(vmem, vmem, vmem),
        scratch_shapes=list(scratch.values()),
        compiler_params=pltpu.CompilerParams(
            collective_id=0, has_side_effects=True, vmem_limit_bytes=62 * 1024 * 1024
        ),
    )(hidden, w_down, w_enc, w_dec, row_list[None], b_enc[None], b_dec, alive_mask[None])
    return (
        latent.reshape(-1, latents),
        residual.reshape(1, -1, width),
        adjoint.reshape(-1, latents),
    )


def solution(mesh):
    return jax.shard_map(
        functools.partial(per_device, digits_of(mesh), mesh.shape["layer"]),
        mesh=mesh,
        in_specs=(
            P("layer", None, "dict"),
            P(),
            P("layer", "dict", None),
            P("layer", None, "dict"),
            P("dict"),
            P("layer", "dict", None),
            P("layer", None),
            P("dict"),
        ),
        out_specs=(P("layer", "dict"), P("layer", "dict", None), P("layer", "dict")),
        check_vma=False,
    )
```

```python
import functools
import itertools
import math

import jax
import jax.numpy as jnp
from jax import lax
from jax.experimental import pallas as pl
from jax.experimental.pallas import tpu as pltpu
from jax.sharding import PartitionSpec as P

F32, BF16, I32 = jnp.float32, jnp.bfloat16, jnp.int32
ORDERS = ((2, 1, 0), (1, 2, 0))
RATE, HOP, LOCAL, MATH = 1e5, 1.5, 6e5, 6e8


def digits_of(mesh):
    line = list(mesh.devices.reshape(mesh.shape["layer"], -1)[0])
    count = len(line)
    try:
        coords = [tuple(d.coords) for d in line]
    except (AttributeError, TypeError):
        coords = None
    sizes = []
    if coords:
        found = []
        for axis in range(len(coords[0])):
            values = [c[axis] for c in coords]
            size = len(set(values))
            if size > 1:
                stride = next(i for i in range(count) if values[i] != values[0])
                found.append((stride, size))
        sizes = [size for _, size in sorted(found, reverse=True)]
    if math.prod(sizes) != count or len(sizes) > 3:
        sizes = [count // 4, 2, 2] if count % 4 == 0 else [count]
    return tuple([1] * (3 - len(sizes)) + sizes)


def kernel(dims, layers, batches, pairs, share, depth, width, latents, names, *refs):
    ref = dict(zip(names, refs))
    count = math.prod(dims)
    part = width // (2 * pairs)
    rows = count * share
    per_layer = count // layers
    layer, place = lax.axis_index("layer"), lax.axis_index("dict")
    mine = (place // (dims[1] * dims[2]), place // dims[2] % dims[1], place % dims[2])
    strides = (dims[1] * dims[2], dims[2], 1)
    free, clock, used = {axis: 0.0 for axis in (0, 1, 2, "layer")}, [0.0], [0]
    sent, active, waiting, ended = [], [], [], {}

    def spend(operations):
        clock[0] += 0.1 + operations / MATH

    def busy(link, length, rate):
        free[link] = max(free[link], clock[0]) + length / rate
        return free[link] + HOP

    def peer_of(axis, step):
        other = lax.rem(mine[axis] + step, dims[axis])
        return other, (layer, place + (other - mine[axis]) * strides[axis])

    def layer_peer(step):
        other = lax.rem(layer + step, layers)
        return other, (other, place)

    def send(src, dst, device):
        slot = used[0]
        used[0] += 1
        copy = pltpu.make_async_remote_copy(
            src_ref=src,
            dst_ref=dst,
            send_sem=ref["send"].at[slot],
            recv_sem=ref["recv"].at[slot],
            device_id=device,
            device_id_type=pl.DeviceIdType.MESH,
        )
        copy.start()
        sent.append(copy)
        return copy

    loads = {}
    for slot, name in enumerate(("hidden", "w_down", "w_enc", "w_dec")):
        loads[name] = pltpu.make_async_copy(ref[name].at[0], ref[name + "_v"], ref["load"].at[slot])
        loads[name].start()

    barrier = pltpu.get_barrier_semaphore()
    peers = [peer_of(axis, step)[1] for axis in range(3) for step in range(1, dims[axis])]
    peers += [layer_peer(step)[1] for step in range(1, layers)]
    for device in peers:
        pl.semaphore_signal(barrier, inc=1, device_id=device, device_id_type=pl.DeviceIdType.MESH)

    at = lax.broadcasted_iota(I32, (count * batches * share,) * 2, 0)
    picked = jnp.where(at == ref["row_list"][...], 1.0, 0.0).T.astype(BF16)
    loads["hidden"].wait()
    last = (((1,), (1,)), ((), ()))
    chosen = lax.dot_general(picked, ref["hidden_v"][...], last, preferred_element_type=F32).astype(BF16)
    ref["chosen"][...] = chosen.reshape(count, batches, share, depth)
    loads["w_down"].wait()
    pl.semaphore_wait(barrier, len(peers))

    def block_of(axes):
        return tuple(pl.ds(mine[a], 1) if a in axes else slice(None) for a in range(3))

    def stage_cost(axis, blocks):
        across = (dims[axis] // 2) * ((dims[axis] + 1) // 2)
        return busy(axis, across * 2 * blocks * share * part * 2, RATE)

    def send_stage(key, side, stage, source):
        axis = ORDERS[side][stage]
        copies = []
        for step in range(1, dims[axis]):
            other, device = peer_of(axis, step)
            index = tuple(pl.ds(other, 1) if a == axis else slice(None) for a in range(3))
            copies.append(send(source.at[index], ref[f"in{key}{stage}"].at[step - 1], device))
        left = math.prod(dims[a] for a in ORDERS[side][stage + 1 :])
        return copies, stage_cost(axis, left)

    def add_stage(key, side, stage, copies):
        axis = ORDERS[side][stage]
        own = ref[f"wide{key[:-1]}"] if stage == 0 else ref[f"sum{key[:-1]}{stage - 1}"]
        for copy in copies:
            copy.wait_recv()
        total = own[block_of((axis,))]
        for step in range(dims[axis] - 1):
            total = total + ref[f"in{key}{stage}"][step].astype(F32)
        return total

    def gather_stage(key, side, stage):
        block = ref[f"all{key}"].at[block_of(ORDERS[side][: stage + 1])]
        axis = ORDERS[side][stage]
        copies = [send(block, block, peer_of(axis, step)[1]) for step in range(1, dims[axis])]
        left = math.prod(dims[a] for a in ORDERS[side][stage + 1 :])
        return copies, stage_cost(axis, left)

    def columns_of(pair):
        return slice(pair * 2 * part, (pair + 1) * 2 * part)

    def exchange(b, pair, phase, value, own_block):
        keys = [f"{b}_{pair}{side}{phase}" for side in range(2)]
        state = []
        for side, key in enumerate(keys):
            term = value[:, side * part : (side + 1) * part].reshape(dims + (share, part))
            ref[f"wide{key[:-1]}"][...] = term
            ref[f"narrow{key}"][...] = term.astype(BF16)
            state.append(send_stage(key, side, 0, ref[f"narrow{key}"]))
        for stage in range(2):
            yield max(ready for _, ready in state)
            following = []
            for side, key in enumerate(keys):
                total = add_stage(key, side, stage, state[side][0])
                ref[f"sum{key[:-1]}{stage}"][...] = total
                ref[f"out{key}{stage}"][...] = total.astype(BF16)
                following.append(send_stage(key, side, stage + 1, ref[f"out{key}{stage}"]))
            spend(0)
            state = following
        yield max(ready for _, ready in state)
        following = []
        for side, key in enumerate(keys):
            total = add_stage(key, side, 2, state[side][0]).reshape(share, part)
            start = (2 * pair + side) * part
            block = own_block(f"{b}_{pair}{side}", total, slice(start, start + part))
            ref[f"all{key}"][block_of((0, 1, 2))] = block.reshape(1, 1, 1, share, part)
            following.append(gather_stage(key, side, 2))
        spend(0)
        state = following
        for stage in (1, 0):
            yield max(ready for _, ready in state)
            following = []
            for side, key in enumerate(keys):
                for copy in state[side][0]:
                    copy.wait_recv()
                following.append(gather_stage(key, side, stage))
            state = following
        yield max(ready for _, ready in state)
        for copies, _ in state:
            for copy in copies:
                copy.wait_recv()

    def gathered(b, pair, phase):
        sides = [ref[f"all{b}_{pair}{side}{phase}"][...].reshape(rows, part) for side in range(2)]
        return jnp.concatenate(sides, axis=1)

    def split():
        loads["w_dec"].wait()

        def step(i, carry):
            at = pl.ds(pl.multiple_of(i * 64, 64), 64)
            value = ref["w_dec_v"][at, :]
            high = value.astype(BF16)
            ref["high"][at, :] = high
            ref["low"][at, :] = (value - high.astype(F32)).astype(BF16)
            return carry

        lax.fori_loop(0, latents // 64, step, 0)
        loads["w_enc"].wait()
        spend(1e9)

    alive = ref["alive"][...].astype(F32)

    def count_up(key):
        ended[key] = ended.get(key, 0) + 1
        return ended[key]

    def forward(b, pair):
        lhs = ref["chosen"][:, b].reshape(rows, depth)
        value = jnp.dot(lhs, ref["w_down_v"][:, columns_of(pair)], preferred_element_type=F32)
        spend(2 * rows * depth * 2 * part)
        yield from exchange(b, pair, 0, value, lambda key, total, columns: total.astype(BF16))
        if not ended:
            split()
        term = jnp.dot(gathered(b, pair, 0), ref["w_enc_v"][columns_of(pair), :], preferred_element_type=F32)
        spend(2 * rows * latents * 2 * part)
        encoded = ref[f"encoded{b}"]
        number = count_up((b, 0))
        encoded[...] = term if number == 1 else encoded[...] + term
        if number < pairs:
            return
        copies = [send(encoded, ref[f"encoded_in{b}"].at[s - 1], layer_peer(s)[1]) for s in range(1, layers)]
        yield busy("layer", rows * latents * 4 * (layers - 1), LOCAL)
        for copy in copies:
            copy.wait_recv()
        preact = encoded[...]
        for s in range(layers - 1):
            preact = preact + ref[f"encoded_in{b}"][s]
        preact = preact + ref["b_enc"][...]
        latent = (jnp.maximum(preact, 0.0) * alive).astype(BF16)
        ref[f"latent{b}"][...] = latent.reshape(count, share, latents)
        ref["latent_out"][:, b] = ref[f"latent{b}"][pl.ds(layer * per_layer, per_layer)]
        spend(0)
        waiting.extend(backward(b, later) for later in range(pairs))

    def backward(b, pair):
        left = ref[f"latent{b}"][...].reshape(rows, latents)
        columns = columns_of(pair)
        value = jnp.dot(left, ref["high"][:, columns], preferred_element_type=F32)
        value = value + jnp.dot(left, ref["low"][:, columns], preferred_element_type=F32)
        spend(4 * rows * latents * 2 * part)

        def residual_block(key, total, columns):
            own = ref[f"all{key}0"][block_of((0, 1, 2))].reshape(share, part).astype(F32)
            residual = own - (total + ref["b_dec"][:, columns])
            ref["residual_out"][b, :, columns] = residual
            return residual.astype(BF16)

        yield from exchange(b, pair, 1, value, residual_block)
        wide = gathered(b, pair, 1)
        term = lax.dot_general(wide, ref["high"][:, columns], last, preferred_element_type=F32)
        term = term + lax.dot_general(wide, ref["low"][:, columns], last, preferred_element_type=F32)
        term = term.reshape(count, share, latents)
        spend(4 * rows * latents * 2 * part)
        back = ref[f"back{b}"]
        number = count_up((b, 1))
        back[...] = term if number == 1 else back[...] + term
        if number < pairs:
            return
        copies = []
        for s in range(1, layers):
            other, device = layer_peer(s)
            block = back.at[pl.ds(other * per_layer, per_layer)]
            copies.append(send(block, ref[f"back_in{b}"].at[s - 1], device))
        yield busy("layer", rows * latents * 4 * (layers - 1) // layers, LOCAL)
        for copy in copies:
            copy.wait_recv()
        total = back[pl.ds(layer * per_layer, per_layer)]
        for s in range(layers - 1):
            total = total + ref[f"back_in{b}"][s]
        ref["adjoint_out"][:, b] = -total * alive[None]
        spend(0)

    waiting.extend(forward(b, pair) for b in range(batches) for pair in range(pairs))
    while active or waiting:
        active.sort(key=lambda entry: entry[0])
        if waiting and (not active or max(free[1], free[2]) <= max(active[0][0], clock[0])):
            item = waiting.pop(0)
        else:
            ready, _, item = active.pop(0)
            clock[0] = max(clock[0], ready)
        ready = next(item, None)
        if ready is not None:
            active.append((ready, len(active), item))
    for copy in sent:
        copy.wait_send()


def copy_kernel(first, second, third, first_out, second_out, third_out, sem):
    copies = [
        pltpu.make_async_copy(source, target, sem.at[slot])
        for slot, (source, target) in enumerate(((first, first_out), (second, second_out), (third, third_out)))
    ]
    for copy in copies:
        copy.start()
    for copy in copies:
        copy.wait()


def per_device(dims, layers, hidden, row_list, w_down, w_enc, b_enc, w_dec, b_dec, alive_mask):
    count = math.prod(dims)
    hidden = jnp.swapaxes(hidden, 1, 2)
    _, depth, row_count = hidden.shape
    width, latents = w_enc.shape[1:]
    pairs = 3 if width % 768 == 0 else 1
    part = width // (2 * pairs)
    batches = 2 if row_count // count % 32 == 0 else 1
    share = row_count // count // batches
    rows = count * share

    scratch = {
        "hidden_v": pltpu.VMEM((depth, row_count), BF16),
        "w_down_v": pltpu.VMEM((depth, width), BF16),
        "w_enc_v": pltpu.VMEM((width, latents), BF16),
        "w_dec_v": pltpu.VMEM((latents, width), F32),
        "high": pltpu.VMEM((latents, width), BF16),
        "low": pltpu.VMEM((latents, width), BF16),
        "chosen": pltpu.VMEM((count, batches, share, depth), BF16),
    }
    for b in range(batches):
        scratch[f"encoded{b}"] = pltpu.VMEM((rows, latents), F32)
        scratch[f"encoded_in{b}"] = pltpu.VMEM((max(layers - 1, 1), rows, latents), F32)
        scratch[f"latent{b}"] = pltpu.VMEM((count, share, latents), BF16)
        scratch[f"back{b}"] = pltpu.VMEM((count, share, latents), F32)
        scratch[f"back_in{b}"] = pltpu.VMEM((max(layers - 1, 1), count // layers, share, latents), F32)
        for pair, side in itertools.product(range(pairs), range(2)):
            key = f"{b}_{pair}{side}"
            scratch[f"wide{key}"] = pltpu.VMEM(dims + (share, part), F32)
            for phase in range(2):
                scratch[f"narrow{key}{phase}"] = pltpu.VMEM(dims + (share, part), BF16)
                scratch[f"all{key}{phase}"] = pltpu.VMEM(dims + (share, part), BF16)
            left = list(dims)
            for stage, axis in enumerate(ORDERS[side]):
                left[axis] = 1
                for phase in range(2):
                    shape = (max(dims[axis] - 1, 1), *left, share, part)
                    scratch[f"in{key}{phase}{stage}"] = pltpu.VMEM(shape, BF16)
                    if stage < 2:
                        scratch[f"out{key}{phase}{stage}"] = pltpu.VMEM((*left, share, part), BF16)
                if stage < 2:
                    scratch[f"sum{key}{stage}"] = pltpu.VMEM((*left, share, part), F32)
    copies = 8 * batches * pairs * sum(d - 1 for d in dims) + 2 * batches * (layers - 1)
    scratch["load"] = pltpu.SemaphoreType.DMA((4,))
    scratch["send"] = pltpu.SemaphoreType.DMA((copies,))
    scratch["recv"] = pltpu.SemaphoreType.DMA((copies,))

    names = ("hidden", "w_down", "w_enc", "w_dec", "row_list", "b_enc", "b_dec", "alive")
    names += ("latent_out", "residual_out", "adjoint_out") + tuple(scratch)
    vmem = pl.BlockSpec(memory_space=pltpu.VMEM)
    hbm = pl.BlockSpec(memory_space=pl.ANY)
    own = (count // layers, batches, share, latents)
    latent, residual, adjoint = pl.pallas_call(
        functools.partial(kernel, dims, layers, batches, pairs, share, depth, width, latents, names),
        out_shape=(
            jax.ShapeDtypeStruct(own, BF16),
            jax.ShapeDtypeStruct((batches, share, width), F32),
            jax.ShapeDtypeStruct(own, F32),
        ),
        in_specs=[hbm] * 4 + [vmem] * 4,
        out_specs=(vmem, vmem, vmem),
        scratch_shapes=list(scratch.values()),
        compiler_params=pltpu.CompilerParams(
            collective_id=0, has_side_effects=True, vmem_limit_bytes=62 * 1024 * 1024
        ),
    )(hidden, w_down, w_enc, w_dec, row_list[None], b_enc[None], b_dec, alive_mask[None])
    results = (latent.reshape(-1, latents), residual.reshape(1, -1, width), adjoint.reshape(-1, latents))
    return tuple(
        pl.pallas_call(
            copy_kernel,
            out_shape=tuple(jax.ShapeDtypeStruct(a.shape, a.dtype) for a in results),
            in_specs=[hbm] * 3,
            out_specs=(hbm,) * 3,
            scratch_shapes=[pltpu.SemaphoreType.DMA((3,))],
        )(*results)
    )


def solution(mesh):
    return jax.shard_map(
        functools.partial(per_device, digits_of(mesh), mesh.shape["layer"]),
        mesh=mesh,
        in_specs=(
            P("layer", None, "dict"),
            P(),
            P("layer", "dict", None),
            P("layer", None, "dict"),
            P("dict"),
            P("layer", "dict", None),
            P("layer", None),
            P("dict"),
        ),
        out_specs=(P("layer", "dict"), P("layer", "dict", None), P("layer", "dict")),
        check_vma=False,
    )
```

```python
import functools
import math

import jax
import jax.numpy as jnp
from jax import lax
from jax.experimental import pallas as pl
from jax.experimental.pallas import tpu as pltpu
from jax.sharding import PartitionSpec as P

F32, BF16, I32 = jnp.float32, jnp.bfloat16, jnp.int32
RATE, HOP, LOCAL, MATH = 9e4, 2.0, 6e5, 4e8
SLACK = 1.0


def digits_of(mesh):
    line = list(mesh.devices.reshape(mesh.shape["layer"], -1)[0])
    count = len(line)
    try:
        coords = [tuple(d.coords) for d in line]
    except (AttributeError, TypeError):
        coords = None
    sizes = []
    if coords:
        found = []
        for axis in range(len(coords[0])):
            values = [c[axis] for c in coords]
            size = len(set(values))
            if size > 1:
                stride = next(i for i in range(count) if values[i] != values[0])
                found.append((stride, size))
        sizes = [size for _, size in sorted(found, reverse=True)]
    if math.prod(sizes) != count or len(sizes) > 3:
        sizes = [count // 4, 2, 2] if count % 4 == 0 else [count]
    sizes = [1] * (3 - len(sizes)) + sizes
    if sizes[0] == 4 and sizes[1:] == [2, 2]:
        sizes = [2, 2, 2, 2]
    return tuple(sizes)


def orders_of(dims):
    if len(dims) == 4:
        return ((3, 2, 1, 0), (2, 3, 1, 0), (1, 0, 3, 2))
    return ((2, 1, 0), (1, 2, 0), (0, 2, 1))


def cuts_of(width):
    if width % 768 or width < 2304:
        return (((0, 0, width),),)
    groups, start = [], 0
    for group in range(width // 768):
        kinds = ((2, 256), (0, 256), (1, 256)) if group % 3 < 2 else ((0, 384), (1, 384))
        parts = []
        for kind, columns in kinds:
            parts.append((kind, start, columns))
            start += columns
        groups.append(tuple(parts))
    return tuple(groups)


def kernel(dims, cuts, layers, batches, share, depth, width, latents, names, *refs):
    ref = dict(zip(names, refs))
    count = math.prod(dims)
    orders, axes = orders_of(dims), range(len(dims))
    pairs = len(cuts)
    rows = count * share
    per_layer = count // layers
    layer, place = lax.axis_index("layer"), lax.axis_index("dict")
    strides = tuple(math.prod(dims[axis + 1 :]) for axis in axes)
    mine = tuple(place // strides[axis] % dims[axis] for axis in axes)
    free, clock, used = {link: 0.0 for link in (*axes, "middle", "layer")}, [0.0], [0]
    sent, active, waiting, ended = [], [], [], {}

    def spend(operations):
        clock[0] += 0.1 + operations / MATH

    def busy(link, length, rate):
        free[link] = max(free[link], clock[0]) + length / rate
        return free[link] + HOP

    def peer_of(axis, step):
        other = lax.rem(mine[axis] + step, dims[axis])
        return other, (layer, place + (other - mine[axis]) * strides[axis])

    def layer_peer(step):
        other = lax.rem(layer + step, layers)
        return other, (other, place)

    def send(src, dst, device):
        slot = used[0]
        used[0] += 1
        copy = pltpu.make_async_remote_copy(
            src_ref=src,
            dst_ref=dst,
            send_sem=ref["send"].at[slot],
            recv_sem=ref["recv"].at[slot],
            device_id=device,
            device_id_type=pl.DeviceIdType.MESH,
        )
        copy.start()
        sent.append(copy)
        return copy

    loads = {}
    for slot, name in enumerate(("hidden", "w_down", "w_enc", "w_dec")):
        loads[name] = pltpu.make_async_copy(ref[name].at[0], ref[name + "_v"], ref["load"].at[slot])
    loads["hidden"].start()
    loads["w_down"].start()

    barrier = pltpu.get_barrier_semaphore()
    peers = [peer_of(axis, step)[1] for axis in axes for step in range(1, dims[axis])]
    peers += [layer_peer(step)[1] for step in range(1, layers)]
    for device in peers:
        pl.semaphore_signal(barrier, inc=1, device_id=device, device_id_type=pl.DeviceIdType.MESH)

    at = lax.broadcasted_iota(I32, (count * batches * share,) * 2, 0)
    picked = jnp.where(at == ref["row_list"][...], 1.0, 0.0).T.astype(BF16)
    ref["picked"][...] = picked.reshape(count, batches, share, count * batches * share)
    last = (((1,), (1,)), ((), ()))
    loads["hidden"].wait()
    loads["w_down"].wait()
    loads["w_enc"].start()
    loads["w_dec"].start()
    pl.semaphore_wait(barrier, len(peers))

    def block_of(among):
        return tuple(pl.ds(mine[a], 1) if a in among else slice(None) for a in axes)

    def stage_cost(axis, blocks, columns):
        length = 2 * blocks * share * columns * 2
        if len(dims) == 4 and axis < 2:
            ready = busy(1, length, RATE)
            return ready if axis else max(ready, busy("middle", 2 * length, RATE))
        return busy(axis, length * (dims[axis] // 2) * ((dims[axis] + 1) // 2), RATE)

    def send_stage(key, part, stage, source):
        kind, _, columns = part
        axis = orders[kind][stage]
        copies = []
        for step in range(1, dims[axis]):
            other, device = peer_of(axis, step)
            index = tuple(pl.ds(other, 1) if a == axis else slice(None) for a in axes)
            copies.append(send(source.at[index], ref[f"in{key}{stage}"].at[step - 1], device))
        left = math.prod(dims[a] for a in orders[kind][stage + 1 :])
        return copies, stage_cost(axis, left, columns)

    def add_stage(key, part, stage, copies):
        axis = orders[part[0]][stage]
        own = ref[f"wide{key[:-1]}"] if stage == 0 else ref[f"sum{key[:-1]}{stage - 1}"]
        for copy in copies:
            copy.wait_recv()
        total = own[block_of((axis,))]
        for step in range(dims[axis] - 1):
            total = total + ref[f"in{key}{stage}"][step].astype(F32)
        return total

    def gather_stage(key, part, stage):
        kind, _, columns = part
        block = ref[f"all{key}"].at[block_of(orders[kind][: stage + 1])]
        axis = orders[kind][stage]
        copies = [send(block, block, peer_of(axis, step)[1]) for step in range(1, dims[axis])]
        left = math.prod(dims[a] for a in orders[kind][stage + 1 :])
        return copies, stage_cost(axis, left, columns)

    def columns_of(pair):
        return slice(cuts[pair][0][1], cuts[pair][-1][1] + cuts[pair][-1][2])

    def exchange(b, pair, phase, value, own_block):
        parts = [(f"{b}_{pair}{side}{phase}", part) for side, part in enumerate(cuts[pair])]
        state, final = [], len(dims) - 1
        for key, part in parts:
            start = part[1] - cuts[pair][0][1]
            term = value[:, start : start + part[2]].reshape(dims + (share, part[2]))
            ref[f"wide{key[:-1]}"][...] = term
            ref[f"narrow{key}"][...] = term.astype(BF16)
            state.append(send_stage(key, part, 0, ref[f"narrow{key}"]))
        for stage in range(final):
            yield max(ready for _, ready in state)
            following = []
            for (key, part), (copies, _) in zip(parts, state):
                total = add_stage(key, part, stage, copies)
                ref[f"out{key}{stage}"][...] = total.astype(BF16)
                following.append(send_stage(key, part, stage + 1, ref[f"out{key}{stage}"]))
                ref[f"sum{key[:-1]}{stage}"][...] = total
            spend(0)
            state = following
        yield max(ready for _, ready in state)
        following = []
        for (key, part), (copies, _) in zip(parts, state):
            total = add_stage(key, part, final, copies).reshape(share, part[2])
            block = own_block(key[:-1], total, slice(part[1], part[1] + part[2]))
            ref[f"all{key}"][block_of(axes)] = block.reshape((1,) * len(dims) + (share, part[2]))
            following.append(gather_stage(key, part, final))
        spend(0)
        state = following
        for stage in reversed(range(final)):
            yield max(ready for _, ready in state)
            following = []
            for (key, part), (copies, _) in zip(parts, state):
                for copy in copies:
                    copy.wait_recv()
                following.append(gather_stage(key, part, stage))
            state = following
        yield max(ready for _, ready in state)
        for copies, _ in state:
            for copy in copies:
                copy.wait_recv()

    def gathered(b, pair, phase):
        sides = [
            ref[f"all{b}_{pair}{side}{phase}"][...].reshape(rows, part[2]) for side, part in enumerate(cuts[pair])
        ]
        return jnp.concatenate(sides, axis=1)

    def split():
        loads["w_dec"].wait()

        def step(i, carry):
            at = pl.ds(pl.multiple_of(i * 64, 64), 64)
            value = ref["w_dec_v"][at, :]
            high = value.astype(BF16)
            ref["high"][at, :] = high
            ref["low"][at, :] = (value - high.astype(F32)).astype(BF16)
            return carry

        lax.fori_loop(0, latents // 64, step, 0)
        loads["w_enc"].wait()
        spend(1e9)

    alive = ref["alive"][...].astype(F32)

    def count_up(key):
        ended[key] = ended.get(key, 0) + 1
        return ended[key]

    def forward(b, pair):
        columns = columns_of(pair)
        span = columns.stop - columns.start
        if pair == 0:
            picked = ref["picked"][:, b].reshape(rows, count * batches * share)
            chosen = lax.dot_general(picked, ref["hidden_v"][...], last, preferred_element_type=F32)
            ref[f"chosen{b}"][...] = chosen.astype(BF16)
            spend(2 * rows * depth * count * batches * share)
        lhs = ref[f"chosen{b}"][...]
        value = jnp.dot(lhs, ref["w_down_v"][:, columns], preferred_element_type=F32)
        spend(2 * rows * depth * span)
        yield from exchange(b, pair, 0, value, lambda key, total, columns: total.astype(BF16))
        if not ended:
            split()
        term = jnp.dot(gathered(b, pair, 0), ref["w_enc_v"][columns, :], preferred_element_type=F32)
        spend(2 * rows * latents * span)
        encoded = ref[f"encoded{b}"]
        number = count_up((b, 0))
        encoded[...] = term if number == 1 else encoded[...] + term
        if number < pairs:
            return
        copies = [send(encoded, ref[f"encoded_in{b}"].at[s - 1], layer_peer(s)[1]) for s in range(1, layers)]
        yield busy("layer", rows * latents * 4 * (layers - 1), LOCAL)
        for copy in copies:
            copy.wait_recv()
        preact = encoded[...]
        for s in range(layers - 1):
            preact = preact + ref[f"encoded_in{b}"][s]
        preact = preact + ref["b_enc"][...]
        latent = (jnp.maximum(preact, 0.0) * alive).astype(BF16)
        ref[f"latent{b}"][...] = latent.reshape(count, share, latents)
        ref["latent_out"][:, b] = ref[f"latent{b}"][pl.ds(layer * per_layer, per_layer)]
        spend(0)
        waiting.extend(backward(b, later) for later in range(pairs))

    def backward(b, pair):
        left = ref[f"latent{b}"][...].reshape(rows, latents)
        columns = columns_of(pair)
        span = columns.stop - columns.start
        value = jnp.dot(left, ref["high"][:, columns], preferred_element_type=F32)
        value = value + jnp.dot(left, ref["low"][:, columns], preferred_element_type=F32)
        spend(4 * rows * latents * span)

        def residual_block(key, total, columns):
            own = ref[f"all{key}0"][block_of(axes)].reshape(total.shape).astype(F32)
            residual = own - (total + ref["b_dec"][:, columns])
            ref["residual_out"][b, :, columns] = residual
            return residual.astype(BF16)

        yield from exchange(b, pair, 1, value, residual_block)
        wide = gathered(b, pair, 1)
        term = lax.dot_general(wide, ref["high"][:, columns], last, preferred_element_type=F32)
        term = term + lax.dot_general(wide, ref["low"][:, columns], last, preferred_element_type=F32)
        term = term.reshape(count, share, latents)
        spend(4 * rows * latents * span)
        back = ref[f"back{b}"]
        number = count_up((b, 1))
        back[...] = term if number == 1 else back[...] + term
        if number < pairs:
            return
        copies = []
        for s in range(1, layers):
            other, device = layer_peer(s)
            block = back.at[pl.ds(other * per_layer, per_layer)]
            copies.append(send(block, ref[f"back_in{b}"].at[s - 1], device))
        yield busy("layer", rows * latents * 4 * (layers - 1) // layers, LOCAL)
        for copy in copies:
            copy.wait_recv()
        total = back[pl.ds(layer * per_layer, per_layer)]
        for s in range(layers - 1):
            total = total + ref[f"back_in{b}"][s]
        ref["adjoint_out"][:, b] = -total * alive[None]
        spend(0)

    waiting.extend(forward(b, pair) for b in range(batches) for pair in range(pairs))
    while active or waiting:
        active.sort(key=lambda entry: entry[0])
        if waiting and (not active or max(free[orders[0][0]], free[orders[1][0]]) <= max(active[0][0], clock[0]) + SLACK):
            item = waiting.pop(0)
        else:
            ready, _, item = active.pop(0)
            clock[0] = max(clock[0], ready)
        ready = next(item, None)
        if ready is not None:
            active.append((ready, len(active), item))
    for copy in sent:
        copy.wait_send()


def copy_kernel(*refs):
    for source, target in zip(refs[:3], refs[3:]):
        target[...] = source[...]


def per_device(dims, layers, hidden, row_list, w_down, w_enc, b_enc, w_dec, b_dec, alive_mask):
    count = math.prod(dims)
    hidden = jnp.swapaxes(hidden, 1, 2)
    _, depth, row_count = hidden.shape
    width, latents = w_enc.shape[1:]
    cuts, orders = cuts_of(width), orders_of(dims)
    batches = 2 if row_count // count % 32 == 0 else 1
    share = row_count // count // batches
    rows = count * share

    scratch = {
        "hidden_v": pltpu.VMEM((depth, row_count), BF16),
        "w_down_v": pltpu.VMEM((depth, width), BF16),
        "w_enc_v": pltpu.VMEM((width, latents), BF16),
        "w_dec_v": pltpu.VMEM((latents, width), F32),
        "high": pltpu.VMEM((latents, width), BF16),
        "low": pltpu.VMEM((latents, width), BF16),
        "picked": pltpu.VMEM((count, batches, share, row_count), BF16),
    }
    for b in range(batches):
        scratch[f"chosen{b}"] = pltpu.VMEM((rows, depth), BF16)
        scratch[f"encoded{b}"] = pltpu.VMEM((rows, latents), F32)
        scratch[f"encoded_in{b}"] = pltpu.VMEM((max(layers - 1, 1), rows, latents), F32)
        scratch[f"latent{b}"] = pltpu.VMEM((count, share, latents), BF16)
        scratch[f"back{b}"] = pltpu.VMEM((count, share, latents), F32)
        scratch[f"back_in{b}"] = pltpu.VMEM((max(layers - 1, 1), count // layers, share, latents), F32)
        for pair, side in [(pair, side) for pair, parts in enumerate(cuts) for side in range(len(parts))]:
            key = f"{b}_{pair}{side}"
            kind, _, part = cuts[pair][side]
            scratch[f"wide{key}"] = pltpu.VMEM(dims + (share, part), F32)
            for phase in range(2):
                scratch[f"narrow{key}{phase}"] = pltpu.VMEM(dims + (share, part), BF16)
                scratch[f"all{key}{phase}"] = pltpu.VMEM(dims + (share, part), BF16)
            left = list(dims)
            for stage, axis in enumerate(orders[kind]):
                left[axis] = 1
                for phase in range(2):
                    shape = (max(dims[axis] - 1, 1), *left, share, part)
                    scratch[f"in{key}{phase}{stage}"] = pltpu.VMEM(shape, BF16)
                    if stage < len(dims) - 1:
                        scratch[f"out{key}{phase}{stage}"] = pltpu.VMEM((*left, share, part), BF16)
                if stage < len(dims) - 1:
                    scratch[f"sum{key}{stage}"] = pltpu.VMEM((*left, share, part), F32)
    copies = 4 * batches * sum(map(len, cuts)) * sum(d - 1 for d in dims) + 2 * batches * (layers - 1)
    scratch["load"] = pltpu.SemaphoreType.DMA((4,))
    scratch["send"] = pltpu.SemaphoreType.DMA((copies,))
    scratch["recv"] = pltpu.SemaphoreType.DMA((copies,))

    names = ("hidden", "w_down", "w_enc", "w_dec", "row_list", "b_enc", "b_dec", "alive")
    names += ("latent_out", "residual_out", "adjoint_out") + tuple(scratch)
    vmem = pl.BlockSpec(memory_space=pltpu.VMEM)
    hbm = pl.BlockSpec(memory_space=pl.ANY)
    own = (count // layers, batches, share, latents)
    latent, residual, adjoint = pl.pallas_call(
        functools.partial(kernel, dims, cuts, layers, batches, share, depth, width, latents, names),
        out_shape=(
            jax.ShapeDtypeStruct(own, BF16),
            jax.ShapeDtypeStruct((batches, share, width), F32),
            jax.ShapeDtypeStruct(own, F32),
        ),
        in_specs=[hbm] * 4 + [vmem] * 4,
        out_specs=(vmem, vmem, vmem),
        scratch_shapes=list(scratch.values()),
        compiler_params=pltpu.CompilerParams(
            collective_id=0, has_side_effects=True, vmem_limit_bytes=62 * 1024 * 1024
        ),
    )(hidden, w_down, w_enc, w_dec, row_list[None], b_enc[None], b_dec, alive_mask[None])
    results = (latent.reshape(-1, latents), residual.reshape(1, -1, width), adjoint.reshape(-1, latents))
    return tuple(
        pl.pallas_call(
            copy_kernel,
            out_shape=tuple(jax.ShapeDtypeStruct(a.shape, a.dtype) for a in results),
            in_specs=[vmem] * 3,
            out_specs=(vmem,) * 3,
        )(*results)
    )


def solution(mesh):
    return jax.shard_map(
        functools.partial(per_device, digits_of(mesh), mesh.shape["layer"]),
        mesh=mesh,
        in_specs=(
            P("layer", None, "dict"),
            P(),
            P("layer", "dict", None),
            P("layer", None, "dict"),
            P("dict"),
            P("layer", "dict", None),
            P("layer", None),
            P("dict"),
        ),
        out_specs=(P("layer", "dict"), P("layer", "dict", None), P("layer", "dict")),
        check_vma=False,
    )
```

```python
import functools
import math

import jax
import jax.numpy as jnp
from jax import lax
from jax.experimental import pallas as pl
from jax.experimental.pallas import tpu as pltpu
from jax.sharding import PartitionSpec as P

F32, BF16, I32 = jnp.float32, jnp.bfloat16, jnp.int32
RATE, HOP, LOCAL, MATH = 9e4, 2.0, 6e5, 4e8
SLACK = 1.0


def digits_of(mesh):
    line = list(mesh.devices.reshape(mesh.shape["layer"], -1)[0])
    count = len(line)
    try:
        coords = [tuple(d.coords) for d in line]
    except (AttributeError, TypeError):
        coords = None
    sizes = []
    if coords:
        found = []
        for axis in range(len(coords[0])):
            values = [c[axis] for c in coords]
            size = len(set(values))
            if size > 1:
                stride = next(i for i in range(count) if values[i] != values[0])
                found.append((stride, size))
        sizes = [size for _, size in sorted(found, reverse=True)]
    if math.prod(sizes) != count or len(sizes) > 3:
        sizes = [count // 4, 2, 2] if count % 4 == 0 else [count]
    sizes = [1] * (3 - len(sizes)) + sizes
    if sizes[0] == 4 and sizes[1:] == [2, 2]:
        sizes = [2, 2, 2, 2]
    return tuple(sizes)


def orders_of(dims):
    if len(dims) == 4:
        return ((3, 2, 1, 0), (2, 3, 1, 0), (1, 0, 3, 2))
    return ((2, 1, 0), (1, 2, 0), (0, 2, 1))


def cuts_of(width):
    if width % 768 or width < 2304:
        return (((0, 0, width),),)
    groups, start = [], 0
    for group in range(width // 768):
        kinds = ((2, 256), (0, 256), (1, 256)) if group % 3 < 2 else ((0, 384), (1, 384))
        parts = []
        for kind, columns in kinds:
            parts.append((kind, start, columns))
            start += columns
        groups.append(tuple(parts))
    return tuple(groups)


def kernel(dims, cuts, layers, batches, share, depth, width, latents, names, *refs):
    ref = dict(zip(names, refs))
    count = math.prod(dims)
    orders, axes = orders_of(dims), range(len(dims))
    pairs = len(cuts)
    rows = count * share
    per_layer = count // layers
    layer, place = lax.axis_index("layer"), lax.axis_index("dict")
    strides = tuple(math.prod(dims[axis + 1 :]) for axis in axes)
    mine = tuple(place // strides[axis] % dims[axis] for axis in axes)
    free, clock, used = {link: 0.0 for link in (*axes, "middle", "layer")}, [0.0], [0]
    sent, active, waiting, ended = [], [], [], {}

    def spend(operations):
        clock[0] += 0.1 + operations / MATH

    def busy(link, length, rate):
        free[link] = max(free[link], clock[0]) + length / rate
        return free[link] + HOP

    def peer_of(axis, step):
        other = lax.rem(mine[axis] + step, dims[axis])
        return other, (layer, place + (other - mine[axis]) * strides[axis])

    def layer_peer(step):
        other = lax.rem(layer + step, layers)
        return other, (other, place)

    def send(src, dst, device):
        slot = used[0]
        used[0] += 1
        copy = pltpu.make_async_remote_copy(
            src_ref=src,
            dst_ref=dst,
            send_sem=ref["send"].at[slot],
            recv_sem=ref["recv"].at[slot],
            device_id=device,
            device_id_type=pl.DeviceIdType.MESH,
        )
        copy.start()
        sent.append(copy)
        return copy

    loads = {}
    for slot, name in enumerate(("hidden", "w_down", "w_enc", "w_dec")):
        loads[name] = pltpu.make_async_copy(ref[name].at[0], ref[name + "_v"], ref["load"].at[slot])
    loads["hidden"].start()
    loads["w_down"].start()

    barrier = pltpu.get_barrier_semaphore()
    peers = [peer_of(axis, step)[1] for axis in axes for step in range(1, dims[axis])]
    peers += [layer_peer(step)[1] for step in range(1, layers)]
    for device in peers:
        pl.semaphore_signal(barrier, inc=1, device_id=device, device_id_type=pl.DeviceIdType.MESH)

    at = lax.broadcasted_iota(I32, (count * batches * share,) * 2, 0)
    picked = jnp.where(at == ref["row_list"][...], 1.0, 0.0).T.astype(BF16)
    ref["picked"][...] = picked.reshape(count, batches, share, count * batches * share)
    last = (((1,), (1,)), ((), ()))
    loads["hidden"].wait()
    loads["w_down"].wait()
    loads["w_enc"].start()
    loads["w_dec"].start()
    pl.semaphore_wait(barrier, len(peers))

    def block_of(kind, stages):
        return tuple(pl.ds(mine[a], 1) if i in stages else slice(None) for i, a in enumerate(orders[kind]))

    def places(kind):
        return [
            tuple(block // strides[a] % dims[a] for a in orders[kind]) for block in range(count)
        ]

    def stage_cost(axis, blocks, columns):
        length = 2 * blocks * share * columns * 2
        if len(dims) == 4 and axis < 2:
            ready = busy(1, length, RATE)
            return ready if axis else max(ready, busy("middle", 2 * length, RATE))
        return busy(axis, length * (dims[axis] // 2) * ((dims[axis] + 1) // 2), RATE)

    def send_stage(key, part, stage, source):
        kind, _, columns = part
        axis = orders[kind][stage]
        copies = []
        for step in range(1, dims[axis]):
            other, device = peer_of(axis, step)
            index = tuple(pl.ds(other, 1) if i == stage else slice(None) for i in axes)
            copies.append(send(source.at[index], ref[f"in{key}{stage}"].at[step - 1], device))
        left = math.prod(dims[a] for a in orders[kind][stage + 1 :])
        return copies, stage_cost(axis, left, columns)

    def add_stage(key, part, stage, copies):
        axis = orders[part[0]][stage]
        own = ref[f"wide{key[:-1]}"] if stage == 0 else ref[f"sum{key[:-1]}{stage - 1}"]
        for copy in copies:
            copy.wait_recv()
        total = own[block_of(part[0], (stage,))]
        for step in range(dims[axis] - 1):
            total = total + ref[f"in{key}{stage}"][step].astype(F32)
        return total

    def gather_stage(key, part, stage):
        kind, _, columns = part
        block = ref[f"all{key}"].at[block_of(kind, range(stage + 1))]
        axis = orders[kind][stage]
        copies = [send(block, block, peer_of(axis, step)[1]) for step in range(1, dims[axis])]
        left = math.prod(dims[a] for a in orders[kind][stage + 1 :])
        return copies, stage_cost(axis, left, columns)

    def columns_of(pair):
        return slice(cuts[pair][0][1], cuts[pair][-1][1] + cuts[pair][-1][2])

    def exchange(b, pair, phase, value, own_block):
        parts = [(f"{b}_{pair}{side}{phase}", part) for side, part in enumerate(cuts[pair])]
        state, final = [], len(dims) - 1
        for key, part in parts:
            start = part[1] - cuts[pair][0][1]
            for block, at in enumerate(places(part[0])):
                term = value[block * share : (block + 1) * share, start : start + part[2]]
                ref[f"wide{key[:-1]}"][at] = term
                ref[f"narrow{key}"][at] = term.astype(BF16)
            state.append(send_stage(key, part, 0, ref[f"narrow{key}"]))
        for stage in range(final):
            yield max(ready for _, ready in state)
            following = []
            for (key, part), (copies, _) in zip(parts, state):
                total = add_stage(key, part, stage, copies)
                ref[f"out{key}{stage}"][...] = total.astype(BF16)
                following.append(send_stage(key, part, stage + 1, ref[f"out{key}{stage}"]))
                ref[f"sum{key[:-1]}{stage}"][...] = total
            spend(0)
            state = following
        yield max(ready for _, ready in state)
        following = []
        for (key, part), (copies, _) in zip(parts, state):
            total = add_stage(key, part, final, copies).reshape(share, part[2])
            index = block_of(part[0], axes)
            block = own_block(key[:-1], index, total, slice(part[1], part[1] + part[2]))
            ref[f"all{key}"][index] = block.reshape((1,) * len(dims) + (share, part[2]))
            following.append(gather_stage(key, part, final))
        spend(0)
        state = following
        for stage in reversed(range(final)):
            yield max(ready for _, ready in state)
            following = []
            for (key, part), (copies, _) in zip(parts, state):
                for copy in copies:
                    copy.wait_recv()
                following.append(gather_stage(key, part, stage))
            state = following
        yield max(ready for _, ready in state)
        for copies, _ in state:
            for copy in copies:
                copy.wait_recv()

    def gathered(b, pair, phase):
        sides = [
            jnp.concatenate([ref[f"all{b}_{pair}{side}{phase}"][at] for at in places(part[0])], axis=0)
            for side, part in enumerate(cuts[pair])
        ]
        return jnp.concatenate(sides, axis=1)

    def split():
        loads["w_dec"].wait()

        def step(i, carry):
            at = pl.ds(pl.multiple_of(i * 64, 64), 64)
            value = ref["w_dec_v"][at, :]
            high = value.astype(BF16)
            ref["high"][at, :] = high
            ref["low"][at, :] = (value - high.astype(F32)).astype(BF16)
            return carry

        lax.fori_loop(0, latents // 64, step, 0)
        loads["w_enc"].wait()
        spend(1e9)

    alive = ref["alive"][...].astype(F32)

    def count_up(key):
        ended[key] = ended.get(key, 0) + 1
        return ended[key]

    def forward(b, pair):
        columns = columns_of(pair)
        span = columns.stop - columns.start
        if pair == 0:
            picked = ref["picked"][:, b].reshape(rows, count * batches * share)
            chosen = lax.dot_general(picked, ref["hidden_v"][...], last, preferred_element_type=F32)
            ref[f"chosen{b}"][...] = chosen.astype(BF16)
            spend(2 * rows * depth * count * batches * share)
        lhs = ref[f"chosen{b}"][...]
        value = jnp.dot(lhs, ref["w_down_v"][:, columns], preferred_element_type=F32)
        spend(2 * rows * depth * span)
        yield from exchange(b, pair, 0, value, lambda key, index, total, columns: total.astype(BF16))
        if not ended:
            split()
        term = jnp.dot(gathered(b, pair, 0), ref["w_enc_v"][columns, :], preferred_element_type=F32)
        spend(2 * rows * latents * span)
        encoded = ref[f"encoded{b}"]
        number = count_up((b, 0))
        encoded[...] = term if number == 1 else encoded[...] + term
        if number < pairs:
            return
        copies = [send(encoded, ref[f"encoded_in{b}"].at[s - 1], layer_peer(s)[1]) for s in range(1, layers)]
        yield busy("layer", rows * latents * 4 * (layers - 1), LOCAL)
        for copy in copies:
            copy.wait_recv()
        preact = encoded[...]
        for s in range(layers - 1):
            preact = preact + ref[f"encoded_in{b}"][s]
        preact = preact + ref["b_enc"][...]
        latent = (jnp.maximum(preact, 0.0) * alive).astype(BF16)
        ref[f"latent{b}"][...] = latent.reshape(count, share, latents)
        ref["latent_out"][:, b] = ref[f"latent{b}"][pl.ds(layer * per_layer, per_layer)]
        spend(0)
        waiting.extend((later, backward(b, later)) for later in range(pairs))

    def backward(b, pair):
        left = ref[f"latent{b}"][...].reshape(rows, latents)
        columns = columns_of(pair)
        span = columns.stop - columns.start
        value = jnp.dot(left, ref["high"][:, columns], preferred_element_type=F32)
        value = value + jnp.dot(left, ref["low"][:, columns], preferred_element_type=F32)
        spend(4 * rows * latents * span)

        def residual_block(key, index, total, columns):
            own = ref[f"all{key}0"][index].reshape(total.shape).astype(F32)
            residual = own - (total + ref["b_dec"][:, columns])
            ref["residual_out"][b, :, columns] = residual
            return residual.astype(BF16)

        yield from exchange(b, pair, 1, value, residual_block)
        wide = gathered(b, pair, 1)
        term = lax.dot_general(wide, ref["high"][:, columns], last, preferred_element_type=F32)
        term = term + lax.dot_general(wide, ref["low"][:, columns], last, preferred_element_type=F32)
        term = term.reshape(count, share, latents)
        spend(4 * rows * latents * span)
        back = ref[f"back{b}"]
        number = count_up((b, 1))
        back[...] = term if number == 1 else back[...] + term
        if number < pairs:
            return
        copies = []
        for s in range(1, layers):
            other, device = layer_peer(s)
            block = back.at[pl.ds(other * per_layer, per_layer)]
            copies.append(send(block, ref[f"back_in{b}"].at[s - 1], device))
        yield busy("layer", rows * latents * 4 * (layers - 1) // layers, LOCAL)
        for copy in copies:
            copy.wait_recv()
        total = back[pl.ds(layer * per_layer, per_layer)]
        for s in range(layers - 1):
            total = total + ref[f"back_in{b}"][s]
        ref["adjoint_out"][:, b] = -total * alive[None]
        spend(0)

    def links_free(pair):
        return max(free[orders[kind][0]] for kind, _, _ in cuts[pair])

    waiting.extend((pair, forward(b, pair)) for b in range(batches) for pair in range(pairs))
    while active or waiting:
        active.sort(key=lambda entry: entry[0])
        until = max(active[0][0], clock[0]) + SLACK if active else math.inf
        start = next((entry for entry in waiting if links_free(entry[0]) <= until), None)
        if start:
            waiting.remove(start)
            item = start[1]
        else:
            ready, _, item = active.pop(0)
            clock[0] = max(clock[0], ready)
        ready = next(item, None)
        if ready is not None:
            active.append((ready, len(active), item))
    for copy in sent:
        copy.wait_send()


def copy_kernel(*refs):
    for source, target in zip(refs[:3], refs[3:]):
        target[...] = source[...]


def per_device(dims, layers, hidden, row_list, w_down, w_enc, b_enc, w_dec, b_dec, alive_mask):
    count = math.prod(dims)
    hidden = jnp.swapaxes(hidden, 1, 2)
    _, depth, row_count = hidden.shape
    width, latents = w_enc.shape[1:]
    cuts, orders = cuts_of(width), orders_of(dims)
    batches = 2 if row_count // count % 32 == 0 else 1
    share = row_count // count // batches
    rows = count * share

    scratch = {
        "hidden_v": pltpu.VMEM((depth, row_count), BF16),
        "w_down_v": pltpu.VMEM((depth, width), BF16),
        "w_enc_v": pltpu.VMEM((width, latents), BF16),
        "w_dec_v": pltpu.VMEM((latents, width), F32),
        "high": pltpu.VMEM((latents, width), BF16),
        "low": pltpu.VMEM((latents, width), BF16),
        "picked": pltpu.VMEM((count, batches, share, row_count), BF16),
    }
    for b in range(batches):
        scratch[f"chosen{b}"] = pltpu.VMEM((rows, depth), BF16)
        scratch[f"encoded{b}"] = pltpu.VMEM((rows, latents), F32)
        scratch[f"encoded_in{b}"] = pltpu.VMEM((max(layers - 1, 1), rows, latents), F32)
        scratch[f"latent{b}"] = pltpu.VMEM((count, share, latents), BF16)
        scratch[f"back{b}"] = pltpu.VMEM((count, share, latents), F32)
        scratch[f"back_in{b}"] = pltpu.VMEM((max(layers - 1, 1), count // layers, share, latents), F32)
        for pair, side in [(pair, side) for pair, parts in enumerate(cuts) for side in range(len(parts))]:
            key = f"{b}_{pair}{side}"
            kind, _, part = cuts[pair][side]
            left = [dims[axis] for axis in orders[kind]]
            scratch[f"wide{key}"] = pltpu.VMEM((*left, share, part), F32)
            for phase in range(2):
                scratch[f"narrow{key}{phase}"] = pltpu.VMEM((*left, share, part), BF16)
                scratch[f"all{key}{phase}"] = pltpu.VMEM((*left, share, part), BF16)
            for stage, axis in enumerate(orders[kind]):
                left[stage] = 1
                for phase in range(2):
                    shape = (max(dims[axis] - 1, 1), *left, share, part)
                    scratch[f"in{key}{phase}{stage}"] = pltpu.VMEM(shape, BF16)
                    if stage < len(dims) - 1:
                        scratch[f"out{key}{phase}{stage}"] = pltpu.VMEM((*left, share, part), BF16)
                if stage < len(dims) - 1:
                    scratch[f"sum{key}{stage}"] = pltpu.VMEM((*left, share, part), F32)
    copies = 4 * batches * sum(map(len, cuts)) * sum(d - 1 for d in dims) + 2 * batches * (layers - 1)
    scratch["load"] = pltpu.SemaphoreType.DMA((4,))
    scratch["send"] = pltpu.SemaphoreType.DMA((copies,))
    scratch["recv"] = pltpu.SemaphoreType.DMA((copies,))

    names = ("hidden", "w_down", "w_enc", "w_dec", "row_list", "b_enc", "b_dec", "alive")
    names += ("latent_out", "residual_out", "adjoint_out") + tuple(scratch)
    vmem = pl.BlockSpec(memory_space=pltpu.VMEM)
    hbm = pl.BlockSpec(memory_space=pl.ANY)
    own = (count // layers, batches, share, latents)
    latent, residual, adjoint = pl.pallas_call(
        functools.partial(kernel, dims, cuts, layers, batches, share, depth, width, latents, names),
        out_shape=(
            jax.ShapeDtypeStruct(own, BF16),
            jax.ShapeDtypeStruct((batches, share, width), F32),
            jax.ShapeDtypeStruct(own, F32),
        ),
        in_specs=[hbm] * 4 + [vmem] * 4,
        out_specs=(vmem, vmem, vmem),
        scratch_shapes=list(scratch.values()),
        compiler_params=pltpu.CompilerParams(
            collective_id=0, has_side_effects=True, vmem_limit_bytes=62 * 1024 * 1024
        ),
    )(hidden, w_down, w_enc, w_dec, row_list[None], b_enc[None], b_dec, alive_mask[None])
    results = (latent.reshape(-1, latents), residual.reshape(1, -1, width), adjoint.reshape(-1, latents))
    return tuple(
        pl.pallas_call(
            copy_kernel,
            out_shape=tuple(jax.ShapeDtypeStruct(a.shape, a.dtype) for a in results),
            in_specs=[vmem] * 3,
            out_specs=(vmem,) * 3,
        )(*results)
    )


def solution(mesh):
    return jax.shard_map(
        functools.partial(per_device, digits_of(mesh), mesh.shape["layer"]),
        mesh=mesh,
        in_specs=(
            P("layer", None, "dict"),
            P(),
            P("layer", "dict", None),
            P("layer", None, "dict"),
            P("dict"),
            P("layer", "dict", None),
            P("layer", None),
            P("dict"),
        ),
        out_specs=(P("layer", "dict"), P("layer", "dict", None), P("layer", "dict")),
        check_vma=False,
    )
```

```python
import functools
import math

import jax
import jax.numpy as jnp
from jax import lax
from jax.experimental import pallas as pl
from jax.experimental.pallas import tpu as pltpu
from jax.sharding import PartitionSpec as P

F32, BF16, I32 = jnp.float32, jnp.bfloat16, jnp.int32
RATE, HOP, LOCAL, MATH = 9e4, 2.0, 6e5, 4e8
SLACK = 1.0


def digits_of(mesh):
    line = list(mesh.devices.reshape(mesh.shape["layer"], -1)[0])
    count = len(line)
    try:
        coords = [tuple(d.coords) for d in line]
    except (AttributeError, TypeError):
        coords = None
    sizes = []
    if coords:
        found = []
        for axis in range(len(coords[0])):
            values = [c[axis] for c in coords]
            size = len(set(values))
            if size > 1:
                stride = next(i for i in range(count) if values[i] != values[0])
                found.append((stride, size))
        sizes = [size for _, size in sorted(found, reverse=True)]
    if math.prod(sizes) != count or len(sizes) > 3:
        sizes = [count // 4, 2, 2] if count % 4 == 0 else [count]
    sizes = [1] * (3 - len(sizes)) + sizes
    if sizes[0] == 4 and sizes[1:] == [2, 2]:
        sizes = [2, 2, 2, 2]
    return tuple(sizes)


def orders_of(dims):
    if len(dims) == 4:
        return ((3, 2, 1, 0), (2, 3, 1, 0), (1, 0, 3, 2))
    return ((2, 1, 0), (1, 2, 0), (0, 2, 1))


def cuts_of(width):
    if width % 2304:
        return (((0, 0, width),),)
    three, two, short = ((2, 256), (0, 256), (1, 256)), ((0, 256), (1, 256)), ((0, 128), (1, 128))
    groups, start = [], 0
    for kinds in (three, two, three, short) * (width // 2304):
        parts = []
        for kind, columns in kinds:
            parts.append((kind, start, columns))
            start += columns
        groups.append(tuple(parts))
    return tuple(groups)


def kernel(dims, cuts, layers, batches, share, depth, width, latents, names, *refs):
    ref = dict(zip(names, refs))
    count = math.prod(dims)
    orders, axes = orders_of(dims), range(len(dims))
    pairs = len(cuts)
    rows = count * share
    per_layer = count // layers
    layer, place = lax.axis_index("layer"), lax.axis_index("dict")
    strides = tuple(math.prod(dims[axis + 1 :]) for axis in axes)
    mine = tuple(place // strides[axis] % dims[axis] for axis in axes)
    free, clock, used = {link: 0.0 for link in (*axes, "middle", "layer")}, [0.0], [0]
    sent, active, waiting, ended = [], [], [], {}

    def spend(operations):
        clock[0] += 0.1 + operations / MATH

    def busy(link, length, rate):
        free[link] = max(free[link], clock[0]) + length / rate
        return free[link] + HOP

    def peer_of(axis, step):
        other = lax.rem(mine[axis] + step, dims[axis])
        return other, (layer, place + (other - mine[axis]) * strides[axis])

    def layer_peer(step):
        other = lax.rem(layer + step, layers)
        return other, (other, place)

    def send(src, dst, device):
        slot = used[0]
        used[0] += 1
        copy = pltpu.make_async_remote_copy(
            src_ref=src,
            dst_ref=dst,
            send_sem=ref["send"].at[slot],
            recv_sem=ref["recv"].at[slot],
            device_id=device,
            device_id_type=pl.DeviceIdType.MESH,
        )
        copy.start()
        sent.append(copy)
        return copy

    loads = {}
    for slot, name in enumerate(("hidden", "w_down", "w_enc", "w_dec")):
        loads[name] = pltpu.make_async_copy(ref[name].at[0], ref[name + "_v"], ref["load"].at[slot])
    loads["hidden"].start()
    loads["w_down"].start()

    barrier = pltpu.get_barrier_semaphore()
    peers = [peer_of(axis, step)[1] for axis in axes for step in range(1, dims[axis])]
    peers += [layer_peer(step)[1] for step in range(1, layers)]
    for device in peers:
        pl.semaphore_signal(barrier, inc=1, device_id=device, device_id_type=pl.DeviceIdType.MESH)

    at = lax.broadcasted_iota(I32, (count * batches * share,) * 2, 0)
    picked = jnp.where(at == ref["row_list"][...], 1.0, 0.0).T.astype(BF16)
    ref["picked"][...] = picked.reshape(count, batches, share, count * batches * share)
    last = (((1,), (1,)), ((), ()))
    loads["hidden"].wait()
    loads["w_down"].wait()
    loads["w_enc"].start()
    loads["w_dec"].start()
    pl.semaphore_wait(barrier, len(peers))

    def block_of(kind, stages):
        return tuple(pl.ds(mine[a], 1) if i in stages else slice(None) for i, a in enumerate(orders[kind]))

    def places(kind):
        return [
            tuple(block // strides[a] % dims[a] for a in orders[kind]) for block in range(count)
        ]

    def stage_cost(axis, blocks, columns):
        length = 2 * blocks * share * columns * 2
        if len(dims) == 4 and axis < 2:
            ready = busy(1, length, RATE)
            return ready if axis else max(ready, busy("middle", 2 * length, RATE))
        return busy(axis, length * (dims[axis] // 2) * ((dims[axis] + 1) // 2), RATE)

    def send_stage(key, part, stage, source):
        kind, _, columns = part
        axis = orders[kind][stage]
        copies = []
        for step in range(1, dims[axis]):
            other, device = peer_of(axis, step)
            index = tuple(pl.ds(other, 1) if i == stage else slice(None) for i in axes)
            copies.append(send(source.at[index], ref[f"in{key}{stage}"].at[step - 1], device))
        left = math.prod(dims[a] for a in orders[kind][stage + 1 :])
        return copies, stage_cost(axis, left, columns)

    def add_stage(key, part, stage, copies):
        axis = orders[part[0]][stage]
        own = ref[f"wide{key[:-1]}"] if stage == 0 else ref[f"sum{key[:-1]}{stage - 1}"]
        for copy in copies:
            copy.wait_recv()
        total = own[block_of(part[0], (stage,))]
        for step in range(dims[axis] - 1):
            total = total + ref[f"in{key}{stage}"][step].astype(F32)
        return total

    def gather_stage(key, part, stage):
        kind, _, columns = part
        block = ref[f"all{key}"].at[block_of(kind, range(stage + 1))]
        axis = orders[kind][stage]
        copies = [send(block, block, peer_of(axis, step)[1]) for step in range(1, dims[axis])]
        left = math.prod(dims[a] for a in orders[kind][stage + 1 :])
        return copies, stage_cost(axis, left, columns)

    def columns_of(pair):
        return slice(cuts[pair][0][1], cuts[pair][-1][1] + cuts[pair][-1][2])

    def exchange(b, pair, phase, value, own_block):
        parts = [(f"{b}_{pair}{side}{phase}", part) for side, part in enumerate(cuts[pair])]
        state, final = [], len(dims) - 1
        for key, part in parts:
            start = part[1] - cuts[pair][0][1]
            for block, at in enumerate(places(part[0])):
                term = value[block * share : (block + 1) * share, start : start + part[2]]
                ref[f"wide{key[:-1]}"][at] = term
                ref[f"narrow{key}"][at] = term.astype(BF16)
            state.append(send_stage(key, part, 0, ref[f"narrow{key}"]))
        for stage in range(final):
            yield max(ready for _, ready in state)
            following = []
            for (key, part), (copies, _) in zip(parts, state):
                total = add_stage(key, part, stage, copies)
                ref[f"out{key}{stage}"][...] = total.astype(BF16)
                following.append(send_stage(key, part, stage + 1, ref[f"out{key}{stage}"]))
                ref[f"sum{key[:-1]}{stage}"][...] = total
            spend(0)
            state = following
        yield max(ready for _, ready in state)
        following = []
        for (key, part), (copies, _) in zip(parts, state):
            total = add_stage(key, part, final, copies).reshape(share, part[2])
            index = block_of(part[0], axes)
            block = own_block(key[:-1], index, total, slice(part[1], part[1] + part[2]))
            ref[f"all{key}"][index] = block.reshape((1,) * len(dims) + (share, part[2]))
            following.append(gather_stage(key, part, final))
        spend(0)
        state = following
        for stage in reversed(range(final)):
            yield max(ready for _, ready in state)
            following = []
            for (key, part), (copies, _) in zip(parts, state):
                for copy in copies:
                    copy.wait_recv()
                following.append(gather_stage(key, part, stage))
            state = following
        yield max(ready for _, ready in state)
        for copies, _ in state:
            for copy in copies:
                copy.wait_recv()

    def gathered(b, pair, phase):
        sides = [
            jnp.concatenate([ref[f"all{b}_{pair}{side}{phase}"][at] for at in places(part[0])], axis=0)
            for side, part in enumerate(cuts[pair])
        ]
        return jnp.concatenate(sides, axis=1)

    def split():
        loads["w_dec"].wait()

        def step(i, carry):
            at = pl.ds(pl.multiple_of(i * 64, 64), 64)
            value = ref["w_dec_v"][at, :]
            high = value.astype(BF16)
            ref["high"][at, :] = high
            ref["low"][at, :] = (value - high.astype(F32)).astype(BF16)
            return carry

        lax.fori_loop(0, latents // 64, step, 0)
        loads["w_enc"].wait()
        spend(1e9)

    alive = ref["alive"][...].astype(F32)

    def count_up(key):
        ended[key] = ended.get(key, 0) + 1
        return ended[key]

    def forward(b, pair):
        columns = columns_of(pair)
        span = columns.stop - columns.start
        if pair == 0:
            picked = ref["picked"][:, b].reshape(rows, count * batches * share)
            chosen = lax.dot_general(picked, ref["hidden_v"][...], last, preferred_element_type=F32)
            ref[f"chosen{b}"][...] = chosen.astype(BF16)
            spend(2 * rows * depth * count * batches * share)
        lhs = ref[f"chosen{b}"][...]
        value = jnp.dot(lhs, ref["w_down_v"][:, columns], preferred_element_type=F32)
        spend(2 * rows * depth * span)
        steps = exchange(b, pair, 0, value, lambda key, index, total, columns: total.astype(BF16))
        first = next(steps)
        if b == 0 and pair == min(1, pairs - 1):
            split()
        yield first
        yield from steps
        term = jnp.dot(gathered(b, pair, 0), ref["w_enc_v"][columns, :], preferred_element_type=F32)
        spend(2 * rows * latents * span)
        encoded = ref[f"encoded{b}"]
        number = count_up((b, 0))
        encoded[...] = term if number == 1 else encoded[...] + term
        if number < pairs:
            return
        copies = [send(encoded, ref[f"encoded_in{b}"].at[s - 1], layer_peer(s)[1]) for s in range(1, layers)]
        yield busy("layer", rows * latents * 4 * (layers - 1), LOCAL)
        for copy in copies:
            copy.wait_recv()
        preact = encoded[...]
        for s in range(layers - 1):
            preact = preact + ref[f"encoded_in{b}"][s]
        preact = preact + ref["b_enc"][...]
        latent = (jnp.maximum(preact, 0.0) * alive).astype(BF16)
        ref[f"latent{b}"][...] = latent.reshape(count, share, latents)
        ref["latent_out"][:, b] = ref[f"latent{b}"][pl.ds(layer * per_layer, per_layer)]
        spend(0)
        waiting.extend((later, backward(b, later)) for later in range(pairs))

    def backward(b, pair):
        left = ref[f"latent{b}"][...].reshape(rows, latents)
        columns = columns_of(pair)
        span = columns.stop - columns.start
        value = jnp.dot(left, ref["high"][:, columns], preferred_element_type=F32)
        value = value + jnp.dot(left, ref["low"][:, columns], preferred_element_type=F32)
        spend(4 * rows * latents * span)

        def residual_block(key, index, total, columns):
            own = ref[f"all{key}0"][index].reshape(total.shape).astype(F32)
            residual = own - (total + ref["b_dec"][:, columns])
            ref["residual_out"][b, :, columns] = residual
            return residual.astype(BF16)

        yield from exchange(b, pair, 1, value, residual_block)
        wide = gathered(b, pair, 1)
        term = lax.dot_general(wide, ref["high"][:, columns], last, preferred_element_type=F32)
        term = term + lax.dot_general(wide, ref["low"][:, columns], last, preferred_element_type=F32)
        term = term.reshape(count, share, latents)
        spend(4 * rows * latents * span)
        back = ref[f"back{b}"]
        number = count_up((b, 1))
        back[...] = term if number == 1 else back[...] + term
        if number < pairs:
            return
        copies = []
        for s in range(1, layers):
            other, device = layer_peer(s)
            block = back.at[pl.ds(other * per_layer, per_layer)]
            copies.append(send(block, ref[f"back_in{b}"].at[s - 1], device))
        yield busy("layer", rows * latents * 4 * (layers - 1) // layers, LOCAL)
        for copy in copies:
            copy.wait_recv()
        total = back[pl.ds(layer * per_layer, per_layer)]
        for s in range(layers - 1):
            total = total + ref[f"back_in{b}"][s]
        ref["adjoint_out"][:, b] = -total * alive[None]
        spend(0)

    def links_free(pair):
        return max(free[orders[kind][0]] for kind, _, _ in cuts[pair])

    waiting.extend((pair, forward(b, pair)) for b in range(batches) for pair in range(pairs))
    while active or waiting:
        active.sort(key=lambda entry: entry[0])
        until = max(active[0][0], clock[0]) + SLACK if active else math.inf
        start = next((entry for entry in waiting if links_free(entry[0]) <= until), None)
        if start:
            waiting.remove(start)
            item = start[1]
        else:
            ready, _, item = active.pop(0)
            clock[0] = max(clock[0], ready)
        ready = next(item, None)
        if ready is not None:
            active.append((ready, len(active), item))
    for copy in sent:
        copy.wait_send()


def copy_kernel(*refs):
    for source, target in zip(refs[:3], refs[3:]):
        target[...] = source[...]


def per_device(dims, layers, hidden, row_list, w_down, w_enc, b_enc, w_dec, b_dec, alive_mask):
    count = math.prod(dims)
    hidden = jnp.swapaxes(hidden, 1, 2)
    _, depth, row_count = hidden.shape
    width, latents = w_enc.shape[1:]
    cuts, orders = cuts_of(width), orders_of(dims)
    batches = 2 if row_count // count % 32 == 0 else 1
    share = row_count // count // batches
    rows = count * share

    scratch = {
        "hidden_v": pltpu.VMEM((depth, row_count), BF16),
        "w_down_v": pltpu.VMEM((depth, width), BF16),
        "w_enc_v": pltpu.VMEM((width, latents), BF16),
        "w_dec_v": pltpu.VMEM((latents, width), F32),
        "high": pltpu.VMEM((latents, width), BF16),
        "low": pltpu.VMEM((latents, width), BF16),
        "picked": pltpu.VMEM((count, batches, share, row_count), BF16),
    }
    for b in range(batches):
        scratch[f"chosen{b}"] = pltpu.VMEM((rows, depth), BF16)
        scratch[f"encoded{b}"] = pltpu.VMEM((rows, latents), F32)
        scratch[f"encoded_in{b}"] = pltpu.VMEM((max(layers - 1, 1), rows, latents), F32)
        scratch[f"latent{b}"] = pltpu.VMEM((count, share, latents), BF16)
        scratch[f"back{b}"] = pltpu.VMEM((count, share, latents), F32)
        scratch[f"back_in{b}"] = pltpu.VMEM((max(layers - 1, 1), count // layers, share, latents), F32)
        for pair, side in [(pair, side) for pair, parts in enumerate(cuts) for side in range(len(parts))]:
            key = f"{b}_{pair}{side}"
            kind, _, part = cuts[pair][side]
            left = [dims[axis] for axis in orders[kind]]
            scratch[f"wide{key}"] = pltpu.VMEM((*left, share, part), F32)
            for phase in range(2):
                scratch[f"narrow{key}{phase}"] = pltpu.VMEM((*left, share, part), BF16)
                scratch[f"all{key}{phase}"] = pltpu.VMEM((*left, share, part), BF16)
            for stage, axis in enumerate(orders[kind]):
                left[stage] = 1
                for phase in range(2):
                    shape = (max(dims[axis] - 1, 1), *left, share, part)
                    scratch[f"in{key}{phase}{stage}"] = pltpu.VMEM(shape, BF16)
                    if stage < len(dims) - 1:
                        scratch[f"out{key}{phase}{stage}"] = pltpu.VMEM((*left, share, part), BF16)
                if stage < len(dims) - 1:
                    scratch[f"sum{key}{stage}"] = pltpu.VMEM((*left, share, part), F32)
    copies = 4 * batches * sum(map(len, cuts)) * sum(d - 1 for d in dims) + 2 * batches * (layers - 1)
    scratch["load"] = pltpu.SemaphoreType.DMA((4,))
    scratch["send"] = pltpu.SemaphoreType.DMA((copies,))
    scratch["recv"] = pltpu.SemaphoreType.DMA((copies,))

    names = ("hidden", "w_down", "w_enc", "w_dec", "row_list", "b_enc", "b_dec", "alive")
    names += ("latent_out", "residual_out", "adjoint_out") + tuple(scratch)
    vmem = pl.BlockSpec(memory_space=pltpu.VMEM)
    hbm = pl.BlockSpec(memory_space=pl.ANY)
    own = (count // layers, batches, share, latents)
    latent, residual, adjoint = pl.pallas_call(
        functools.partial(kernel, dims, cuts, layers, batches, share, depth, width, latents, names),
        out_shape=(
            jax.ShapeDtypeStruct(own, BF16),
            jax.ShapeDtypeStruct((batches, share, width), F32),
            jax.ShapeDtypeStruct(own, F32),
        ),
        in_specs=[hbm] * 4 + [vmem] * 4,
        out_specs=(vmem, vmem, vmem),
        scratch_shapes=list(scratch.values()),
        compiler_params=pltpu.CompilerParams(
            collective_id=0, has_side_effects=True, vmem_limit_bytes=62 * 1024 * 1024
        ),
    )(hidden, w_down, w_enc, w_dec, row_list[None], b_enc[None], b_dec, alive_mask[None])
    results = (latent.reshape(-1, latents), residual.reshape(1, -1, width), adjoint.reshape(-1, latents))
    return tuple(
        pl.pallas_call(
            copy_kernel,
            out_shape=tuple(jax.ShapeDtypeStruct(a.shape, a.dtype) for a in results),
            in_specs=[vmem] * 3,
            out_specs=(vmem,) * 3,
        )(*results)
    )


def solution(mesh):
    return jax.shard_map(
        functools.partial(per_device, digits_of(mesh), mesh.shape["layer"]),
        mesh=mesh,
        in_specs=(
            P("layer", None, "dict"),
            P(),
            P("layer", "dict", None),
            P("layer", None, "dict"),
            P("dict"),
            P("layer", "dict", None),
            P("layer", None),
            P("dict"),
        ),
        out_specs=(P("layer", "dict"), P("layer", "dict", None), P("layer", "dict")),
        check_vma=False,
    )
```
